32 devices in a mesh: grp: 2 (over y), gx: 16 (over z, x, core).
Axes of the slice: x: 2, y: 2, z: 4, core: 2. Of those that a mesh axis runs over, the one named last changes fastest.
Arguments:
- features: bfloat16 [128, 32, 64, 128], P('grp', 'gx'), parts along dimension 0, may hold values from -6 to 6
- cotangent: bfloat16 [128, 32, 64, 128], P('grp', 'gx'), parts along dimension 0, may hold values from -6 to 6
- spectral_weight: bfloat16 [16384, 64, 128], P('gx'), may hold values from -0.5 to 0.5
- channel_weight: bfloat16 [64, 64], replicated, may hold values from -0.75 to 0.75
- channel_bias: float32 [64], replicated, may hold values from -3 to 3
Outputs:
- activated: bfloat16 [128, 32, 64, 128], P('grp', 'gx'), parts along dimension 0
- feature_grad: bfloat16 [128, 32, 64, 128], P('grp', 'gx'), parts along dimension 0
- spectral_grad: bfloat16 [32768, 64, 128], P(('grp', 'gx')), parts along dimension 0
The draws below stay inside these ranges and needn't reach their ends.
There are 2 independent parts, one for each index of `grp`. The reference program is written for one: setup_inputs(seed, part) draws one part's arguments, and reference() takes and returns one part's arrays. A program takes and returns all parts, laid end to end along the dimension named above; an argument that names none is the same for every part. Nothing has to cross between parts.
All inputs are finite; a program needn't handle non-finite values.
Results may differ from the reference program's by a relative error of at most 0.018.
Values may be sent and summed in bfloat16 or wider, within the bound.
A program may use at most 192 MiB of HBM per device.

```python
import math
import jax
import jax.numpy as jnp

C = 64
MX = 32
MY = 32
MZ = 16
NZ = 128
NY = 64
NX = 32
MODES = 16384


def level_of(stream_key, extent, shards, low, largest):
    def one(axis_at, shards_of):
        heights = jax.random.uniform(jax.random.fold_in(jax.random.fold_in(stream_key, 6), axis_at), (shards_of,), jnp.float32, low / len(shards), largest / len(shards))
        return jnp.repeat(jnp.exp(heights), extent[axis_at] // shards_of).reshape((-1,) + (1,) * (len(extent) - axis_at - 1))

    factor_of = one(*shards[0])
    for cut in shards[1:]:
        factor_of = factor_of * one(*cut)
    return factor_of


def noise(own_key, dims, scale, most, split=(), held_as=jnp.bfloat16):
    result = scale * jax.random.normal(own_key, dims, jnp.float32)
    if split:
        result = result * level_of(own_key, dims, split, -0.22, 0.18)
    return jnp.clip(result, -most, most).astype(held_as)


def setup_inputs(seed: int = 0, part: int = 0) -> dict:
    streams_of = jax.random.split(jax.random.key(seed), 6)
    own_keys = jax.random.split(jax.random.fold_in(streams_of[5], part), 6)
    return {
        "features": noise(own_keys[0], (C, NX, NY, NZ), 1.0, 6.0, ((1, 16),)),
        "cotangent": noise(own_keys[1], (C, NX, NY, NZ), 1.0, 6.0, ((1, 16),)),
        "spectral_weight": noise(streams_of[2], (MODES, C, 2 * C), (2 * C) ** -0.5, 0.5, ((0, 16),)),
        "channel_weight": noise(streams_of[3], (C, C), C ** -0.5, 0.75),
        "channel_bias": noise(streams_of[4], (C,), 0.5, 3.0, (), jnp.float32),
    }


SQRT_TWO_PI = math.sqrt(2.0 / math.pi)
CUBIC_COEF = 0.044715

def freq_index(retained, length):
    ladder = jnp.arange(retained, dtype=jnp.int32)
    return jnp.where(ladder < retained // 2, ladder, length - retained + ladder).astype(jnp.int32)

def cos_sin(wavenum, length):
    points = jnp.arange(length, dtype=jnp.int32)
    angles = (wavenum[:, None] * points[None, :] % length).astype(jnp.float32) * (2.0 * math.pi / length)
    return (jnp.cos(angles), jnp.sin(angles))

def analysis_pair(wavenum, length):
    cosine, sine_wave = cos_sin(wavenum, length)
    cosine, sine_wave = (cosine.T, sine_wave.T)
    return jnp.stack([jnp.stack([cosine, -sine_wave], 1), jnp.stack([sine_wave, cosine], 1)], 1).astype(jnp.bfloat16)

def synthesis_pair(wavenum, length):
    cosine, sine_wave = cos_sin(wavenum, length)
    return jnp.stack([jnp.stack([cosine, sine_wave], 1), jnp.stack([-sine_wave, cosine], 1)], 1).astype(jnp.bfloat16)

def depth_table(retained, length):
    cosine, sine_wave = cos_sin(jnp.arange(retained, dtype=jnp.int32), length)
    return jnp.concatenate([cosine, -sine_wave], 0).astype(jnp.bfloat16)

def gelu_parts(inputs):
    cubed_in = inputs * inputs * inputs
    tangent = jnp.tanh(SQRT_TWO_PI * (inputs + CUBIC_COEF * cubed_in))
    output = 0.5 * inputs * (1.0 + tangent)
    derivative = 0.5 * (1.0 + tangent) + 0.5 * inputs * (1.0 - tangent * tangent) * SQRT_TWO_PI * (1.0 + 3.0 * CUBIC_COEF * inputs * inputs)
    return (output, derivative)

def mode_product(coeffs, weights, channels):
    stacked = coeffs.reshape(coeffs.shape[0], 2, channels).astype(jnp.float32)
    halves = jnp.einsum('mac,mcj->amj', stacked, weights.astype(jnp.float32))
    real_out = halves[0, :, :channels] - halves[1, :, channels:]
    imag_out = halves[0, :, channels:] + halves[1, :, :channels]
    return jnp.concatenate([real_out, imag_out], 1).astype(jnp.bfloat16)

def mode_grads(coeffs, weights, grad_modes, channels, weight_scale, input_scale):
    number = coeffs.shape[0]
    stacked = coeffs.reshape(number, 2, channels).astype(jnp.float32)
    grad_pairs = grad_modes.reshape(number, 2, channels).astype(jnp.float32)
    real_w = jnp.einsum('mac,mao->mco', stacked, grad_pairs)
    imag_w = jnp.einsum('mc,mo->mco', stacked[:, 0], grad_pairs[:, 1]) - jnp.einsum('mc,mo->mco', stacked[:, 1], grad_pairs[:, 0])
    weight_grad = (jnp.concatenate([real_w, imag_w], 2) * weight_scale).astype(jnp.bfloat16)
    straight = jnp.concatenate([grad_pairs[:, 0], grad_pairs[:, 1]], 1)
    rotated = jnp.concatenate([grad_pairs[:, 1], -grad_pairs[:, 0]], 1)
    wide_weights = weights.astype(jnp.float32)
    real_x = jnp.einsum('mcj,mj->mc', wide_weights, straight)
    imag_x = jnp.einsum('mcj,mj->mc', wide_weights, rotated)
    input_grad = (jnp.concatenate([real_x, imag_x], 1) * input_scale).astype(jnp.bfloat16)
    return (weight_grad, input_grad)

def reference(features, cotangent, spectral_weight, channel_weight, channel_bias):
    wave_pairs = MY * MZ
    forward_scale = 1.0 / math.sqrt(NX * NY * NZ)
    inverse_scale = 1.0 / math.sqrt(MODES)
    weight_scale = math.sqrt(MODES / (NX * NY * NZ))
    depth_basis = depth_table(MZ, NZ)
    across_y = analysis_pair(freq_index(MY, NY), NY).astype(jnp.float32)
    across_x = analysis_pair(freq_index(MX, NX), NX).astype(jnp.float32)
    back_y = synthesis_pair(freq_index(MY, NY), NY).astype(jnp.float32)
    back_x = synthesis_pair(freq_index(MX, NX), NX).astype(jnp.float32)
    depth_part = jnp.dot(features, depth_basis.T, preferred_element_type=jnp.float32).astype(jnp.bfloat16)
    depth_five = depth_part.reshape(C, NX, NY, 2, MZ).astype(jnp.float32)
    plane_part = jnp.einsum('cxyaz,yabk->cxbkz', depth_five, across_y).astype(jnp.bfloat16).reshape(C, NX, 2, wave_pairs)
    mode_sums = jnp.einsum('cxaq,xabk->qkbc', plane_part.astype(jnp.float32), across_x).reshape(MODES, 2 * C)
    coeffs = (mode_sums * forward_scale).astype(jnp.bfloat16)
    mode_block = math.gcd(MODES, 1024)
    spectral_list = []
    for offset in range(0, MODES, mode_block):
        spectral_list.append(mode_product(coeffs[offset:offset + mode_block], spectral_weight[offset:offset + mode_block], C))
    spectral = jnp.concatenate(spectral_list, 0)
    planes_back = jnp.einsum('qkao,kabx->oxbq', spectral.reshape(wave_pairs, MX, 2, C).astype(jnp.float32), back_x).astype(jnp.bfloat16)
    slab_size = math.gcd(NX, 16)
    act_list = []
    upstream_list = []
    rows_list = []
    for offset in range(0, NX, slab_size):
        rows_back = planes_back[:, offset:offset + slab_size].reshape(C, slab_size, 2, MY, MZ).astype(jnp.float32)
        lines_back = jnp.einsum('oxakz,kaby->oxybz', rows_back, back_y).astype(jnp.bfloat16).reshape(C, slab_size, NY, 2 * MZ)
        spectral_term = jnp.dot(lines_back, depth_basis, preferred_element_type=jnp.float32) * inverse_scale
        local_in = features[:, offset:offset + slab_size]
        pointwise = jnp.dot(channel_weight, local_in.reshape(C, -1), preferred_element_type=jnp.float32).reshape(C, slab_size, NY, NZ)
        hidden = spectral_term + pointwise + channel_bias.astype(jnp.float32)[:, None, None, None]
        activated, derivative = gelu_parts(hidden)
        act_list.append(activated.astype(jnp.bfloat16))
        upstream = (cotangent[:, offset:offset + slab_size].astype(jnp.float32) * derivative).astype(jnp.bfloat16)
        upstream_list.append(upstream)
        lines_grad = (jnp.dot(upstream, depth_basis.T, preferred_element_type=jnp.float32) * inverse_scale).astype(jnp.bfloat16)
        lines_five = lines_grad.reshape(C, slab_size, NY, 2, MZ).astype(jnp.float32)
        rows_grad = jnp.einsum('oxybz,kaby->oxakz', lines_five, back_y).astype(jnp.bfloat16).reshape(C, slab_size, 2, wave_pairs)
        rows_list.append(rows_grad)
    activated_all = jnp.concatenate(act_list, 1)
    rows_all = jnp.concatenate(rows_list, 1)
    grad_sums = jnp.einsum('oxbq,kabx->qkao', rows_all.astype(jnp.float32), back_x).reshape(MODES, 2 * C)
    grad_modes = grad_sums.astype(jnp.bfloat16)
    weight_list = []
    coeff_list = []
    for offset in range(0, MODES, mode_block):
        weight_grad, input_grad = mode_grads(coeffs[offset:offset + mode_block], spectral_weight[offset:offset + mode_block], grad_modes[offset:offset + mode_block], C, weight_scale, forward_scale)
        weight_list.append(weight_grad)
        coeff_list.append(input_grad)
    spectral_grad = jnp.concatenate(weight_list, 0)
    coeff_grad = jnp.concatenate(coeff_list, 0)
    plane_grad = jnp.einsum('qkbc,xabk->cxaq', coeff_grad.reshape(wave_pairs, MX, 2, C).astype(jnp.float32), across_x).astype(jnp.bfloat16)
    grad_list = []
    for index_slab, offset in enumerate(range(0, NX, slab_size)):
        block_grad = plane_grad[:, offset:offset + slab_size].reshape(C, slab_size, 2, MY, MZ).astype(jnp.float32)
        depth_grad = jnp.einsum('cxbkz,yabk->cxyaz', block_grad, across_y).astype(jnp.bfloat16).reshape(C, slab_size, NY, 2 * MZ)
        upstream = upstream_list[index_slab]
        channel_back = jnp.dot(channel_weight.T, upstream.reshape(C, -1), preferred_element_type=jnp.float32).reshape(C, slab_size, NY, NZ)
        total_grad = jnp.dot(depth_grad, depth_basis, preferred_element_type=jnp.float32) + channel_back
        grad_list.append(total_grad.astype(jnp.bfloat16))
    feature_grad = jnp.concatenate(grad_list, 1)
    return (activated_all, feature_grad, spectral_grad)
```

```python
import math

import jax
import jax.numpy as jnp
from jax import lax
from jax.sharding import PartitionSpec as P

MX = 32
MY = 32
MZ = 16


SQRT_TWO_PI = math.sqrt(2.0 / math.pi)
CUBIC_COEF = 0.044715


def freq_index(retained, length):
    ladder = jnp.arange(retained, dtype=jnp.int32)
    return jnp.where(ladder < retained // 2, ladder, length - retained + ladder)


def cos_sin(wavenum, length):
    points = jnp.arange(length, dtype=jnp.int32)
    angles = (wavenum[:, None] * points[None, :] % length).astype(jnp.float32) * (
        2.0 * math.pi / length
    )
    return (jnp.cos(angles), jnp.sin(angles))


def analysis_pair(wavenum, length):
    cosine, sine_wave = cos_sin(wavenum, length)
    cosine, sine_wave = (cosine.T, sine_wave.T)
    return jnp.stack(
        [jnp.stack([cosine, -sine_wave], 1), jnp.stack([sine_wave, cosine], 1)], 1
    ).astype(jnp.bfloat16)


def synthesis_pair(wavenum, length):
    cosine, sine_wave = cos_sin(wavenum, length)
    return jnp.stack(
        [jnp.stack([cosine, sine_wave], 1), jnp.stack([-sine_wave, cosine], 1)], 1
    ).astype(jnp.bfloat16)


def depth_table(retained, length):
    cosine, sine_wave = cos_sin(jnp.arange(retained, dtype=jnp.int32), length)
    return jnp.concatenate([cosine, -sine_wave], 0).astype(jnp.bfloat16)


def gelu_parts(inputs):
    cubed_in = inputs * inputs * inputs
    tangent = jnp.tanh(SQRT_TWO_PI * (inputs + CUBIC_COEF * cubed_in))
    output = 0.5 * inputs * (1.0 + tangent)
    derivative = 0.5 * (1.0 + tangent) + 0.5 * inputs * (1.0 - tangent * tangent) * SQRT_TWO_PI * (
        1.0 + 3.0 * CUBIC_COEF * inputs * inputs
    )
    return (output, derivative)


def mode_product(coeffs, weights):
    channels = weights.shape[1]
    halves = jnp.einsum("mac,mcj->amj", coeffs, weights, preferred_element_type=jnp.float32)
    real_out = halves[0, :, :channels] - halves[1, :, channels:]
    imag_out = halves[0, :, channels:] + halves[1, :, :channels]
    return jnp.stack([real_out, imag_out], 1).astype(jnp.bfloat16)


def exchange(blocks):
    return lax.all_to_all(blocks, "gx", 0, 0, tiled=True)


def body(features, cotangent, spectral_weight, channel_weight, channel_bias):
    channels, planes, lines, depth_len = features.shape
    devices = lax.axis_size("gx")
    all_planes = planes * devices
    owned_modes = spectral_weight.shape[0]
    wave_pairs = MY * MZ
    owned_pairs = owned_modes // MX
    wide = 2 * channels
    forward_scale = 1.0 / math.sqrt(all_planes * lines * depth_len)
    inverse_scale = 1.0 / math.sqrt(MX * wave_pairs)
    weight_scale = math.sqrt(MX * wave_pairs / (all_planes * lines * depth_len))
    depth_basis = depth_table(MZ, depth_len)
    across_y = analysis_pair(freq_index(MY, lines), lines)
    back_y = synthesis_pair(freq_index(MY, lines), lines)
    across_x = analysis_pair(freq_index(MX, all_planes), all_planes)
    back_x = synthesis_pair(freq_index(MX, all_planes), all_planes)

    def to_owners(rows):
        blocks = rows.reshape(devices, owned_pairs * planes, wide)
        return exchange(blocks).reshape(devices, owned_pairs, planes, 2, channels)

    def to_planes(rows):
        blocks = rows.reshape(devices, planes * owned_pairs, wide)
        got = exchange(blocks).reshape(devices, planes, owned_pairs, 2, channels)
        return got.transpose(1, 0, 2, 3, 4).reshape(planes, MY, MZ, 2, channels)

    depth_part = jnp.dot(features, depth_basis.T, preferred_element_type=jnp.float32).astype(
        jnp.bfloat16
    )
    plane_part = jnp.einsum(
        "cxyaz,yabk->kzxbc",
        depth_part.reshape(channels, planes, lines, 2, MZ),
        across_y,
        preferred_element_type=jnp.float32,
    ).astype(jnp.bfloat16)
    gathered = to_owners(plane_part)
    mode_sums = jnp.einsum(
        "sqpac,spabk->qkbc",
        gathered,
        across_x.reshape(devices, planes, 2, 2, MX),
        preferred_element_type=jnp.float32,
    )
    coeffs = (mode_sums * forward_scale).astype(jnp.bfloat16).reshape(owned_modes, 2, channels)
    spectral = mode_product(coeffs, spectral_weight)
    planes_back = jnp.einsum(
        "qkao,kabx->xqbo",
        spectral.reshape(owned_pairs, MX, 2, channels),
        back_x,
        preferred_element_type=jnp.float32,
    ).astype(jnp.bfloat16)
    planes_here = to_planes(planes_back)
    lines_back = (
        jnp.einsum("xkzao,kaby->oxybz", planes_here, back_y, preferred_element_type=jnp.float32)
        .astype(jnp.bfloat16)
        .reshape(channels, planes, lines, 2 * MZ)
    )
    spectral_term = (
        jnp.dot(lines_back, depth_basis, preferred_element_type=jnp.float32) * inverse_scale
    )
    pointwise = jnp.einsum(
        "oc,cxyz->oxyz", channel_weight, features, preferred_element_type=jnp.float32
    )
    hidden = spectral_term + pointwise + channel_bias[:, None, None, None]
    activated, derivative = gelu_parts(hidden)
    upstream = (cotangent.astype(jnp.float32) * derivative).astype(jnp.bfloat16)
    lines_grad = (
        jnp.dot(upstream, depth_basis.T, preferred_element_type=jnp.float32) * inverse_scale
    ).astype(jnp.bfloat16)
    rows_grad = jnp.einsum(
        "oxybz,kaby->kzxao",
        lines_grad.reshape(channels, planes, lines, 2, MZ),
        back_y,
        preferred_element_type=jnp.float32,
    ).astype(jnp.bfloat16)
    gathered_grad = to_owners(rows_grad)
    grad_modes = (
        jnp.einsum(
            "sqpbo,kabsp->qkao",
            gathered_grad,
            back_x.reshape(MX, 2, 2, devices, planes),
            preferred_element_type=jnp.float32,
        )
        .astype(jnp.bfloat16)
        .reshape(owned_modes, 2, channels)
    )
    straight = grad_modes.reshape(owned_modes, wide)
    rotated = jnp.concatenate([grad_modes[:, 1], -grad_modes[:, 0]], 1)
    pairs = jnp.stack([straight, rotated], 1)
    coeff_grad = (
        jnp.einsum("mcj,mbj->mbc", spectral_weight, pairs, preferred_element_type=jnp.float32)
        * forward_scale
    ).astype(jnp.bfloat16)
    plane_grad = jnp.einsum(
        "qkbc,xabk->xqac",
        coeff_grad.reshape(owned_pairs, MX, 2, channels),
        across_x,
        preferred_element_type=jnp.float32,
    ).astype(jnp.bfloat16)
    grad_here = to_planes(plane_grad)
    spectral_grad = (
        jnp.einsum("mac,maj->mcj", coeffs, pairs, preferred_element_type=jnp.float32)
        * weight_scale
    ).astype(jnp.bfloat16)
    depth_grad = (
        jnp.einsum("xkzbc,yabk->cxyaz", grad_here, across_y, preferred_element_type=jnp.float32)
        .astype(jnp.bfloat16)
        .reshape(channels, planes, lines, 2 * MZ)
    )
    channel_back = jnp.einsum(
        "oc,oxyz->cxyz", channel_weight, upstream, preferred_element_type=jnp.float32
    )
    feature_grad = (
        jnp.dot(depth_grad, depth_basis, preferred_element_type=jnp.float32) + channel_back
    ).astype(jnp.bfloat16)
    return (activated.astype(jnp.bfloat16), feature_grad, spectral_grad)


def solution(mesh):
    in_specs = (
        P("grp", "gx", None, None),
        P("grp", "gx", None, None),
        P("gx", None, None),
        P(),
        P(),
    )
    out_specs = (
        P("grp", "gx", None, None),
        P("grp", "gx", None, None),
        P(("grp", "gx"), None, None),
    )
    return jax.shard_map(body, mesh=mesh, in_specs=in_specs, out_specs=out_specs, check_vma=False)
```

```python
import functools
import math

import jax
import jax.numpy as jnp
from jax import lax
from jax.experimental import pallas as pl
from jax.experimental.pallas import tpu as pltpu
from jax.sharding import PartitionSpec as P

MX = 32
MY = 32
MZ = 16


SQRT_TWO_PI = math.sqrt(2.0 / math.pi)
CUBIC_COEF = 0.044715


def freq_index(retained, length):
    ladder = jnp.arange(retained, dtype=jnp.int32)
    return jnp.where(ladder < retained // 2, ladder, length - retained + ladder)


def cos_sin(wavenum, length):
    points = jnp.arange(length, dtype=jnp.int32)
    angles = (wavenum[:, None] * points[None, :] % length).astype(jnp.float32) * (
        2.0 * math.pi / length
    )
    return (jnp.cos(angles), jnp.sin(angles))


def analysis_pair(wavenum, length):
    cosine, sine_wave = cos_sin(wavenum, length)
    cosine, sine_wave = (cosine.T, sine_wave.T)
    return jnp.stack(
        [jnp.stack([cosine, -sine_wave], 1), jnp.stack([sine_wave, cosine], 1)], 1
    ).astype(jnp.bfloat16)


def synthesis_pair(wavenum, length):
    cosine, sine_wave = cos_sin(wavenum, length)
    return jnp.stack(
        [jnp.stack([cosine, sine_wave], 1), jnp.stack([-sine_wave, cosine], 1)], 1
    ).astype(jnp.bfloat16)


def depth_table(retained, length):
    cosine, sine_wave = cos_sin(jnp.arange(retained, dtype=jnp.int32), length)
    return jnp.concatenate([cosine, -sine_wave], 0).astype(jnp.bfloat16)


def gelu_parts(inputs):
    cubed_in = inputs * inputs * inputs
    tangent = jnp.tanh(SQRT_TWO_PI * (inputs + CUBIC_COEF * cubed_in))
    output = 0.5 * inputs * (1.0 + tangent)
    derivative = 0.5 * (1.0 + tangent) + 0.5 * inputs * (1.0 - tangent * tangent) * SQRT_TWO_PI * (
        1.0 + 3.0 * CUBIC_COEF * inputs * inputs
    )
    return (output, derivative)


def mode_product(coeffs, weights):
    channels = weights.shape[1]
    halves = jnp.einsum("mac,mcj->amj", coeffs, weights, preferred_element_type=jnp.float32)
    real_out = halves[0, :, :channels] - halves[1, :, channels:]
    imag_out = halves[0, :, channels:] + halves[1, :, :channels]
    return jnp.stack([real_out, imag_out], 1).astype(jnp.bfloat16)


def exchange(blocks):
    return lax.all_to_all(blocks, "gx", 0, 0, tiled=True)


def middle_kernel(
    scale, feat_ref, cot_ref, lines_ref, weight_ref, bias_ref, basis_ref, act_ref, up_ref, grad_ref
):
    channels, _, rows, depth_len = feat_ref.shape
    spectral = jnp.dot(
        lines_ref[0].reshape(rows * channels, lines_ref.shape[3]),
        basis_ref[...],
        preferred_element_type=jnp.float32,
    ).reshape(rows, channels, depth_len)
    feats = jnp.swapaxes(feat_ref[:, 0].astype(jnp.float32), 0, 1).astype(jnp.bfloat16)
    cots = jnp.swapaxes(cot_ref[:, 0].astype(jnp.float32), 0, 1)
    acts = []
    for row in range(rows):
        pointwise = jnp.dot(weight_ref[...], feats[row], preferred_element_type=jnp.float32)
        hidden = spectral[row] * scale + pointwise + bias_ref[...]
        activated, derivative = gelu_parts(hidden)
        acts.append(activated)
        up_ref[0, row] = (cots[row] * derivative).astype(jnp.bfloat16)
    act_ref[:, 0] = jnp.swapaxes(jnp.stack(acts, 0), 0, 1).astype(jnp.bfloat16)
    grad = lax.dot_general(
        up_ref[0].reshape(rows * channels, depth_len),
        basis_ref[...],
        (((1,), (1,)), ((), ())),
        preferred_element_type=jnp.float32,
    )
    grad_ref[0] = (grad * scale).astype(jnp.bfloat16).reshape(rows, channels, lines_ref.shape[3])


def final_kernel(up_ref, depth_ref, weight_ref, basis_ref, out_ref):
    _, rows, channels, depth_len = up_ref.shape
    spectral = jnp.dot(
        depth_ref[0].reshape(rows * channels, depth_ref.shape[3]),
        basis_ref[...],
        preferred_element_type=jnp.float32,
    ).reshape(rows, channels, depth_len)
    totals = []
    for row in range(rows):
        back = jnp.dot(weight_ref[...], up_ref[0, row], preferred_element_type=jnp.float32)
        totals.append(spectral[row] + back)
    out_ref[:, 0] = jnp.swapaxes(jnp.stack(totals, 0), 0, 1).astype(jnp.bfloat16)


ROWS = 16


def middle(features, cotangent, lines_back, channel_weight, channel_bias, depth_basis, scale):
    channels, planes, lines, depth_len = features.shape
    parts = lines_back.shape[3]
    field = pl.BlockSpec((channels, 1, ROWS, depth_len), lambda x, y: (0, x, y, 0))
    turned = pl.BlockSpec((1, ROWS, channels, depth_len), lambda x, y: (x, y, 0, 0))
    narrow = pl.BlockSpec((1, ROWS, channels, parts), lambda x, y: (x, y, 0, 0))
    count = features.size
    return pl.pallas_call(
        functools.partial(middle_kernel, scale),
        grid=(planes, lines // ROWS),
        in_specs=[
            field,
            field,
            narrow,
            pl.BlockSpec((channels, channels), lambda x, y: (0, 0)),
            pl.BlockSpec((channels, 1), lambda x, y: (0, 0)),
            pl.BlockSpec((parts, depth_len), lambda x, y: (0, 0)),
        ],
        out_specs=[field, turned, narrow],
        out_shape=[
            jax.ShapeDtypeStruct(features.shape, jnp.bfloat16),
            jax.ShapeDtypeStruct((planes, lines, channels, depth_len), jnp.bfloat16),
            jax.ShapeDtypeStruct((planes, lines, channels, parts), jnp.bfloat16),
        ],
        compiler_params=pltpu.CompilerParams(vmem_limit_bytes=56 * 1024 * 1024),
        cost_estimate=pl.CostEstimate(
            flops=count * 2 * (channels + 2 * parts), bytes_accessed=count * 8, transcendentals=count
        ),
    )(features, cotangent, lines_back, channel_weight, channel_bias[:, None], depth_basis)


def final(upstream, depth_grad, weight_back, depth_basis):
    planes, lines, channels, depth_len = upstream.shape
    parts = depth_grad.shape[3]
    count = upstream.size
    return pl.pallas_call(
        final_kernel,
        grid=(planes, lines // ROWS),
        in_specs=[
            pl.BlockSpec((1, ROWS, channels, depth_len), lambda x, y: (x, y, 0, 0)),
            pl.BlockSpec((1, ROWS, channels, parts), lambda x, y: (x, y, 0, 0)),
            pl.BlockSpec((channels, channels), lambda x, y: (0, 0)),
            pl.BlockSpec((parts, depth_len), lambda x, y: (0, 0)),
        ],
        out_specs=pl.BlockSpec((channels, 1, ROWS, depth_len), lambda x, y: (0, x, y, 0)),
        out_shape=jax.ShapeDtypeStruct((channels, planes, lines, depth_len), jnp.bfloat16),
        compiler_params=pltpu.CompilerParams(vmem_limit_bytes=32 * 1024 * 1024),
        cost_estimate=pl.CostEstimate(
            flops=count * 2 * (channels + parts), bytes_accessed=count * 4, transcendentals=0
        ),
    )(upstream, depth_grad, weight_back, depth_basis)


def body(features, cotangent, spectral_weight, channel_weight, channel_bias):
    channels, planes, lines, depth_len = features.shape
    devices = lax.axis_size("gx")
    all_planes = planes * devices
    owned_modes = spectral_weight.shape[0]
    wave_pairs = MY * MZ
    owned_pairs = owned_modes // MX
    wide = 2 * channels
    forward_scale = 1.0 / math.sqrt(all_planes * lines * depth_len)
    inverse_scale = 1.0 / math.sqrt(MX * wave_pairs)
    weight_scale = math.sqrt(MX * wave_pairs / (all_planes * lines * depth_len))
    depth_basis = depth_table(MZ, depth_len)
    across_y = analysis_pair(freq_index(MY, lines), lines)
    back_y = synthesis_pair(freq_index(MY, lines), lines)
    across_x = analysis_pair(freq_index(MX, all_planes), all_planes)
    back_x = synthesis_pair(freq_index(MX, all_planes), all_planes)

    def to_owners(rows):
        blocks = rows.reshape(devices, owned_pairs * planes, wide)
        return exchange(blocks).reshape(devices, owned_pairs, planes, 2, channels)

    def to_planes(rows):
        blocks = rows.reshape(devices, planes * owned_pairs, wide)
        got = exchange(blocks).reshape(devices, planes, owned_pairs, 2, channels)
        return got.transpose(1, 0, 2, 3, 4).reshape(planes, MY, MZ, 2, channels)

    depth_part = jnp.dot(features, depth_basis.T, preferred_element_type=jnp.float32).astype(
        jnp.bfloat16
    )
    plane_part = jnp.einsum(
        "cxyaz,yabk->kzxbc",
        depth_part.reshape(channels, planes, lines, 2, MZ),
        across_y,
        preferred_element_type=jnp.float32,
    ).astype(jnp.bfloat16)
    gathered = to_owners(plane_part)
    mode_sums = jnp.einsum(
        "sqpac,spabk->qkbc",
        gathered,
        across_x.reshape(devices, planes, 2, 2, MX),
        preferred_element_type=jnp.float32,
    )
    coeffs = (mode_sums * forward_scale).astype(jnp.bfloat16).reshape(owned_modes, 2, channels)
    spectral = mode_product(coeffs, spectral_weight)
    planes_back = jnp.einsum(
        "qkao,kabx->xqbo",
        spectral.reshape(owned_pairs, MX, 2, channels),
        back_x,
        preferred_element_type=jnp.float32,
    ).astype(jnp.bfloat16)
    planes_here = to_planes(planes_back)
    lines_back = (
        jnp.einsum("xkzao,kaby->xyobz", planes_here, back_y, preferred_element_type=jnp.float32)
        .astype(jnp.bfloat16)
        .reshape(planes, lines, channels, 2 * MZ)
    )
    activated, upstream, lines_grad = middle(
        features, cotangent, lines_back, channel_weight, channel_bias, depth_basis, inverse_scale
    )
    rows_grad = jnp.einsum(
        "xyobz,kaby->kzxao",
        lines_grad.reshape(planes, lines, channels, 2, MZ),
        back_y,
        preferred_element_type=jnp.float32,
    ).astype(jnp.bfloat16)
    gathered_grad = to_owners(rows_grad)
    grad_modes = (
        jnp.einsum(
            "sqpbo,kabsp->qkao",
            gathered_grad,
            back_x.reshape(MX, 2, 2, devices, planes),
            preferred_element_type=jnp.float32,
        )
        .astype(jnp.bfloat16)
        .reshape(owned_modes, 2, channels)
    )
    straight = grad_modes.reshape(owned_modes, wide)
    rotated = jnp.concatenate([grad_modes[:, 1], -grad_modes[:, 0]], 1)
    pairs = jnp.stack([straight, rotated], 1)
    coeff_grad = (
        jnp.einsum("mcj,mbj->mbc", spectral_weight, pairs, preferred_element_type=jnp.float32)
        * forward_scale
    ).astype(jnp.bfloat16)
    plane_grad = jnp.einsum(
        "qkbc,xabk->xqac",
        coeff_grad.reshape(owned_pairs, MX, 2, channels),
        across_x,
        preferred_element_type=jnp.float32,
    ).astype(jnp.bfloat16)
    grad_here = to_planes(plane_grad)
    spectral_grad = (
        jnp.einsum("mac,maj->mcj", coeffs, pairs, preferred_element_type=jnp.float32)
        * weight_scale
    ).astype(jnp.bfloat16)
    depth_grad = (
        jnp.einsum("xkzbc,yabk->xycaz", grad_here, across_y, preferred_element_type=jnp.float32)
        .astype(jnp.bfloat16)
        .reshape(planes, lines, channels, 2 * MZ)
    )
    feature_grad = final(upstream, depth_grad, channel_weight.T, depth_basis)
    return (activated, feature_grad, spectral_grad)


def solution(mesh):
    in_specs = (
        P("grp", "gx", None, None),
        P("grp", "gx", None, None),
        P("gx", None, None),
        P(),
        P(),
    )
    out_specs = (
        P("grp", "gx", None, None),
        P("grp", "gx", None, None),
        P(("grp", "gx"), None, None),
    )
    return jax.shard_map(body, mesh=mesh, in_specs=in_specs, out_specs=out_specs, check_vma=False)
```

```python
import functools
import math

import jax
import jax.numpy as jnp
from jax import lax
from jax.experimental import pallas as pl
from jax.experimental.pallas import tpu as pltpu
from jax.sharding import PartitionSpec as P

MX = 32
MY = 32
MZ = 16


SQRT_TWO_PI = math.sqrt(2.0 / math.pi)
CUBIC_COEF = 0.044715


def freq_index(retained, length):
    ladder = jnp.arange(retained, dtype=jnp.int32)
    return jnp.where(ladder < retained // 2, ladder, length - retained + ladder)


def cos_sin(wavenum, length):
    points = jnp.arange(length, dtype=jnp.int32)
    angles = (wavenum[:, None] * points[None, :] % length).astype(jnp.float32) * (
        2.0 * math.pi / length
    )
    return (jnp.cos(angles), jnp.sin(angles))


def analysis_pair(wavenum, length):
    cosine, sine_wave = cos_sin(wavenum, length)
    cosine, sine_wave = (cosine.T, sine_wave.T)
    return jnp.stack(
        [jnp.stack([cosine, -sine_wave], 1), jnp.stack([sine_wave, cosine], 1)], 1
    ).astype(jnp.bfloat16)


def synthesis_pair(wavenum, length):
    cosine, sine_wave = cos_sin(wavenum, length)
    return jnp.stack(
        [jnp.stack([cosine, sine_wave], 1), jnp.stack([-sine_wave, cosine], 1)], 1
    ).astype(jnp.bfloat16)


def depth_table(retained, length):
    cosine, sine_wave = cos_sin(jnp.arange(retained, dtype=jnp.int32), length)
    return jnp.concatenate([cosine, -sine_wave], 0).astype(jnp.bfloat16)


def gelu_parts(inputs):
    squared = inputs * inputs
    slope = SQRT_TWO_PI * CUBIC_COEF
    tangent = jnp.tanh(inputs * (SQRT_TWO_PI + slope * squared))
    half = 0.5 + 0.5 * tangent
    output = inputs * half
    derivative = half + output * (1.0 - tangent) * (SQRT_TWO_PI + 3.0 * slope * squared)
    return (output, derivative)


def mode_product(coeffs, weights):
    channels = weights.shape[1]
    halves = jnp.einsum("mac,mcj->amj", coeffs, weights, preferred_element_type=jnp.float32)
    real_out = halves[0, :, :channels] - halves[1, :, channels:]
    imag_out = halves[0, :, channels:] + halves[1, :, :channels]
    return jnp.stack([real_out, imag_out], 1).astype(jnp.bfloat16)


def exchange(blocks):
    return lax.all_to_all(blocks, "gx", 0, 0, tiled=True)


def middle_kernel(
    scale, feat_ref, cot_ref, lines_ref, weight_ref, bias_ref, basis_ref, act_ref, up_ref, grad_ref
):
    channels, _, rows, depth_len = feat_ref.shape
    spectral = jnp.dot(
        lines_ref[0].reshape(rows * channels, lines_ref.shape[3]),
        basis_ref[...],
        preferred_element_type=jnp.float32,
    ).reshape(rows, channels, depth_len)
    feats = jnp.swapaxes(feat_ref[:, 0].astype(jnp.float32), 0, 1).astype(jnp.bfloat16)
    cots = jnp.swapaxes(cot_ref[:, 0].astype(jnp.float32), 0, 1)
    acts = []
    for row in range(rows):
        pointwise = jnp.dot(weight_ref[...], feats[row], preferred_element_type=jnp.float32)
        hidden = spectral[row] * scale + pointwise + bias_ref[...]
        activated, derivative = gelu_parts(hidden)
        acts.append(activated)
        up_ref[0, row] = (cots[row] * derivative).astype(jnp.bfloat16)
    act_ref[:, 0] = jnp.swapaxes(jnp.stack(acts, 0), 0, 1).astype(jnp.bfloat16)
    grad = lax.dot_general(
        up_ref[0].reshape(rows * channels, depth_len),
        basis_ref[...],
        (((1,), (1,)), ((), ())),
        preferred_element_type=jnp.float32,
    )
    grad_ref[0] = (grad * scale).astype(jnp.bfloat16).reshape(rows, channels, lines_ref.shape[3])


def final_kernel(up_ref, depth_ref, weight_ref, basis_ref, out_ref):
    _, rows, channels, depth_len = up_ref.shape
    spectral = jnp.dot(
        depth_ref[0].reshape(rows * channels, depth_ref.shape[3]),
        basis_ref[...],
        preferred_element_type=jnp.float32,
    ).reshape(rows, channels, depth_len)
    totals = []
    for row in range(rows):
        back = jnp.dot(weight_ref[...], up_ref[0, row], preferred_element_type=jnp.float32)
        totals.append(spectral[row] + back)
    out_ref[:, 0] = jnp.swapaxes(jnp.stack(totals, 0), 0, 1).astype(jnp.bfloat16)


ROWS = 16


def middle(features, cotangent, lines_back, channel_weight, channel_bias, depth_basis, scale):
    channels, planes, lines, depth_len = features.shape
    parts = lines_back.shape[3]
    field = pl.BlockSpec((channels, 1, ROWS, depth_len), lambda x, y: (0, x, y, 0))
    turned = pl.BlockSpec((1, ROWS, channels, depth_len), lambda x, y: (x, y, 0, 0))
    narrow = pl.BlockSpec((1, ROWS, channels, parts), lambda x, y: (x, y, 0, 0))
    count = features.size
    return pl.pallas_call(
        functools.partial(middle_kernel, scale),
        grid=(planes, lines // ROWS),
        in_specs=[
            field,
            field,
            narrow,
            pl.BlockSpec((channels, channels), lambda x, y: (0, 0)),
            pl.BlockSpec((channels, 1), lambda x, y: (0, 0)),
            pl.BlockSpec((parts, depth_len), lambda x, y: (0, 0)),
        ],
        out_specs=[field, turned, narrow],
        out_shape=[
            jax.ShapeDtypeStruct(features.shape, jnp.bfloat16),
            jax.ShapeDtypeStruct((planes, lines, channels, depth_len), jnp.bfloat16),
            jax.ShapeDtypeStruct((planes, lines, channels, parts), jnp.bfloat16),
        ],
        compiler_params=pltpu.CompilerParams(vmem_limit_bytes=56 * 1024 * 1024),
        cost_estimate=pl.CostEstimate(
            flops=count * 2 * (channels + 2 * parts), bytes_accessed=count * 8, transcendentals=count
        ),
    )(features, cotangent, lines_back, channel_weight, channel_bias[:, None], depth_basis)


def final(upstream, depth_grad, weight_back, depth_basis):
    planes, lines, channels, depth_len = upstream.shape
    parts = depth_grad.shape[3]
    count = upstream.size
    return pl.pallas_call(
        final_kernel,
        grid=(planes, lines // ROWS),
        in_specs=[
            pl.BlockSpec((1, ROWS, channels, depth_len), lambda x, y: (x, y, 0, 0)),
            pl.BlockSpec((1, ROWS, channels, parts), lambda x, y: (x, y, 0, 0)),
            pl.BlockSpec((channels, channels), lambda x, y: (0, 0)),
            pl.BlockSpec((parts, depth_len), lambda x, y: (0, 0)),
        ],
        out_specs=pl.BlockSpec((channels, 1, ROWS, depth_len), lambda x, y: (0, x, y, 0)),
        out_shape=jax.ShapeDtypeStruct((channels, planes, lines, depth_len), jnp.bfloat16),
        compiler_params=pltpu.CompilerParams(vmem_limit_bytes=32 * 1024 * 1024),
        cost_estimate=pl.CostEstimate(
            flops=count * 2 * (channels + parts), bytes_accessed=count * 4, transcendentals=0
        ),
    )(upstream, depth_grad, weight_back, depth_basis)


def body(features, cotangent, spectral_weight, channel_weight, channel_bias):
    channels, planes, lines, depth_len = features.shape
    devices = lax.axis_size("gx")
    all_planes = planes * devices
    owned_modes = spectral_weight.shape[0]
    wave_pairs = MY * MZ
    owned_pairs = owned_modes // MX
    wide = 2 * channels
    forward_scale = 1.0 / math.sqrt(all_planes * lines * depth_len)
    inverse_scale = 1.0 / math.sqrt(MX * wave_pairs)
    weight_scale = math.sqrt(MX * wave_pairs / (all_planes * lines * depth_len))
    depth_basis = depth_table(MZ, depth_len)
    across_y = analysis_pair(freq_index(MY, lines), lines)
    back_y = synthesis_pair(freq_index(MY, lines), lines)
    across_x = analysis_pair(freq_index(MX, all_planes), all_planes)
    back_x = synthesis_pair(freq_index(MX, all_planes), all_planes)

    def to_owners(rows):
        blocks = rows.reshape(devices, owned_pairs * planes, wide)
        return exchange(blocks).reshape(devices, owned_pairs, planes, 2, channels)

    def to_planes(rows):
        blocks = rows.reshape(devices, planes * owned_pairs, wide)
        got = exchange(blocks).reshape(devices, planes, owned_pairs, 2, channels)
        return got.transpose(1, 0, 2, 3, 4).reshape(planes, MY, MZ, 2, channels)

    depth_part = jnp.dot(features, depth_basis.T, preferred_element_type=jnp.float32).astype(
        jnp.bfloat16
    )
    plane_part = jnp.einsum(
        "cxyaz,yabk->kzxbc",
        depth_part.reshape(channels, planes, lines, 2, MZ),
        across_y,
        preferred_element_type=jnp.float32,
    ).astype(jnp.bfloat16)
    gathered = to_owners(plane_part)
    mode_sums = jnp.einsum(
        "sqpac,spabk->qkbc",
        gathered,
        across_x.reshape(devices, planes, 2, 2, MX),
        preferred_element_type=jnp.float32,
    )
    coeffs = (mode_sums * forward_scale).astype(jnp.bfloat16).reshape(owned_modes, 2, channels)
    spectral = mode_product(coeffs, spectral_weight)
    planes_back = jnp.einsum(
        "qkao,kabx->xqbo",
        spectral.reshape(owned_pairs, MX, 2, channels),
        back_x,
        preferred_element_type=jnp.float32,
    ).astype(jnp.bfloat16)
    planes_here = to_planes(planes_back)
    lines_back = (
        jnp.einsum("xkzao,kaby->xyobz", planes_here, back_y, preferred_element_type=jnp.float32)
        .astype(jnp.bfloat16)
        .reshape(planes, lines, channels, 2 * MZ)
    )
    activated, upstream, lines_grad = middle(
        features, cotangent, lines_back, channel_weight, channel_bias, depth_basis, inverse_scale
    )
    rows_grad = jnp.einsum(
        "xyobz,kaby->kzxao",
        lines_grad.reshape(planes, lines, channels, 2, MZ),
        back_y,
        preferred_element_type=jnp.float32,
    ).astype(jnp.bfloat16)
    gathered_grad = to_owners(rows_grad)
    grad_modes = (
        jnp.einsum(
            "sqpbo,kabsp->qkao",
            gathered_grad,
            back_x.reshape(MX, 2, 2, devices, planes),
            preferred_element_type=jnp.float32,
        )
        .astype(jnp.bfloat16)
        .reshape(owned_modes, 2, channels)
    )
    straight = grad_modes.reshape(owned_modes, wide)
    rotated = jnp.concatenate([grad_modes[:, 1], -grad_modes[:, 0]], 1)
    pairs = jnp.stack([straight, rotated], 1)
    coeff_grad = (
        jnp.einsum("mcj,mbj->mbc", spectral_weight, pairs, preferred_element_type=jnp.float32)
        * forward_scale
    ).astype(jnp.bfloat16)
    plane_grad = jnp.einsum(
        "qkbc,xabk->xqac",
        coeff_grad.reshape(owned_pairs, MX, 2, channels),
        across_x,
        preferred_element_type=jnp.float32,
    ).astype(jnp.bfloat16)
    grad_here = to_planes(plane_grad)
    spectral_grad = (
        jnp.einsum("mac,maj->mcj", coeffs, pairs, preferred_element_type=jnp.float32)
        * weight_scale
    ).astype(jnp.bfloat16)
    depth_grad = (
        jnp.einsum("xkzbc,yabk->xycaz", grad_here, across_y, preferred_element_type=jnp.float32)
        .astype(jnp.bfloat16)
        .reshape(planes, lines, channels, 2 * MZ)
    )
    feature_grad = final(upstream, depth_grad, channel_weight.T, depth_basis)
    return (activated, feature_grad, spectral_grad)


def solution(mesh):
    in_specs = (
        P("grp", "gx", None, None),
        P("grp", "gx", None, None),
        P("gx", None, None),
        P(),
        P(),
    )
    out_specs = (
        P("grp", "gx", None, None),
        P("grp", "gx", None, None),
        P(("grp", "gx"), None, None),
    )
    return jax.shard_map(body, mesh=mesh, in_specs=in_specs, out_specs=out_specs, check_vma=False)
```
